32 devices in a mesh: parts: 2 (over y), energy: 4 (over x, core), orb: 4 (over z).
Axes of the slice: x: 2, y: 2, z: 4, core: 2. Of those that a mesh axis runs over, the one named last changes fastest.
Arguments:
- greens: float32 [8, 24, 2, 128, 128], P(('parts', 'energy'), 'orb'), parts along dimension 0, may hold values from -6 to 6
- derivative: bfloat16 [24, 8, 3, 128, 128], P('orb'), may hold values from -0.5 to 0.5
- phonon: float32 [2, 6, 3, 3], replicated, may hold values from -2 to 2
- mode_index: int32 [24, 8], P('orb'), may hold values from 0 to 5
- neighbours: int32 [24, 8], replicated, may hold values from 0 to 23, as said below
- counts: int32 [24], replicated, may hold values from 1 to 8
- shifts: int32 [2], replicated, may hold values from 1 to 3, as said below
Outputs:
- self_energy: float32 [8, 24, 2, 128, 128], P(('parts', 'energy'), 'orb'), parts along dimension 0
The draws below stay inside these ranges and needn't reach their ends.
There are 2 independent parts, one for each index of `parts`. The reference program is written for one: setup_inputs(seed, part) draws one part's arguments, and reference() takes and returns one part's arrays. A program takes and returns all parts, laid end to end along the dimension named above; an argument that names none is the same for every part. Nothing has to cross between parts.
Inputs may be any that keep to these rules, and one draw needn't show every extreme that they name: `neighbours`: for the 6 groups of one orb index, the live slots (k < counts) name groups held by any one orb index at most 12 times, and some pair of orb indices reaches 12; in some orb index every group has all 8 slots live. The two shifts differ.
All inputs are finite; a program needn't handle non-finite values.
Results may differ from the reference program's by a relative error of at most 0.005.
Values may be sent and summed in bfloat16 or wider, within the bound.
A program may use at most 128 MiB of HBM per device.

```python
import jax
import jax.numpy as jnp
from jax import lax

NO = 128
NB = 8
MODES = 6
G_DEV = 6
GROUPS = 24
ENERGIES = 4
N_ORB = 4


def neighbour_tables(key):
    subkeys = jax.random.split(jax.random.fold_in(key, 17), 5)
    counts = jax.random.randint(subkeys[0], (GROUPS,), 1, NB + 1)
    full_reader = jax.random.randint(subkeys[1], (), 0, N_ORB)
    reader_of = jnp.arange(GROUPS) // G_DEV
    counts = jnp.where(reader_of == full_reader, NB, counts).astype(jnp.int32)
    slot_total = G_DEV * NB
    live_slots = (jnp.arange(NB)[None, :] < counts[:, None]).reshape(N_ORB, slot_total)
    live_rank = jnp.cumsum(live_slots.astype(jnp.int32), axis=1) - 1
    reader_keys = jax.random.split(subkeys[2], N_ORB)
    orders = jax.vmap(lambda single: jax.random.permutation(single, N_ORB))(reader_keys)
    owner_live = jnp.take_along_axis(orders, jnp.mod(jnp.maximum(live_rank, 0), N_ORB), axis=1)
    owner_dead = jax.random.randint(subkeys[3], (N_ORB, slot_total), 0, N_ORB)
    owner = jnp.where(live_slots, owner_live, owner_dead)
    local_pick = jax.random.randint(subkeys[4], (N_ORB, slot_total), 0, G_DEV)
    neighbours = (owner * G_DEV + local_pick).reshape(GROUPS, NB).astype(jnp.int32)
    return (neighbours, counts)


def draw_neighbours(key, part):
    return neighbour_tables(key)[0]


def draw_counts(key, part):
    return neighbour_tables(key)[1]


def draw_shifts(key, part):
    key = jax.random.fold_in(key, 29)
    first_key, second_key = jax.random.split(key)
    first_shift = jax.random.randint(first_key, (), 1, ENERGIES).astype(jnp.int32)
    offset = jax.random.randint(second_key, (), 1, ENERGIES - 1).astype(jnp.int32)
    second_shift = 1 + jnp.mod(first_shift - 1 + offset, ENERGIES - 1)
    return jnp.stack([first_shift, second_shift.astype(jnp.int32)]).astype(jnp.int32)


def set_ends(result, own_key, least, high):
    longest = result.shape.index(max(result.shape))
    spots = []
    for shift in (0, 1):
        where = [jax.random.randint(jax.random.fold_in(own_key, axis), (), 0, length) for axis, length in enumerate(result.shape)]
        where[longest] = (where[longest] + shift) % result.shape[longest]
        spots.append(tuple(where))
    return result.at[spots[0]].set(least).at[spots[1]].set(high)


def block_levels(own_key, extent, pieces, smallest, largest):
    def one(axis_at, parts):
        draws = jax.random.uniform(jax.random.fold_in(jax.random.fold_in(own_key, 6), axis_at), (parts,), jnp.float32, smallest / len(pieces), largest / len(pieces))
        return jnp.repeat(jnp.exp(draws), extent[axis_at] // parts).reshape((-1,) + (1,) * (len(extent) - axis_at - 1))

    level = one(*pieces[0])
    for cut in pieces[1:]:
        level = level * one(*cut)
    return level


def scatter_about(stream_key, extent, width, reach, cuts=(), held_as=jnp.bfloat16):
    drawn = width * jax.random.normal(stream_key, extent, jnp.float32)
    if cuts:
        drawn = drawn * block_levels(stream_key, extent, cuts, -0.22, 0.18)
    return jnp.clip(drawn, -reach, reach).astype(held_as)


def setup_inputs(seed: int = 0, part: int = 0) -> dict:
    splits = jax.random.split(jax.random.key(seed), 8)
    part_keys = jax.random.split(jax.random.fold_in(splits[7], part), 8)
    greens = scatter_about(part_keys[0], (ENERGIES, GROUPS, 2, NO, NO), 1.0, 6.0, ((0, 4), (1, 4)), jnp.float32)
    derivative = scatter_about(splits[1], (GROUPS, NB, 3, NO, NO), NO ** -0.5, 0.5, ((0, 4),))
    phonon = scatter_about(splits[2], (2, MODES, 3, 3), 0.35, 2.0, (), jnp.float32)
    mode_index = set_ends(jax.random.randint(splits[3], (GROUPS, NB), 0, MODES), jax.random.fold_in(splits[3], 1), 0, MODES - 1).astype(jnp.int32)
    neighbours = draw_neighbours(jax.random.fold_in(splits[7], 71), part)
    counts = draw_counts(jax.random.fold_in(splits[7], 71), part)
    shifts = draw_shifts(jax.random.fold_in(splits[7], 71), part)
    return {"greens": greens, "derivative": derivative, "phonon": phonon, "mode_index": mode_index, "neighbours": neighbours, "counts": counts, "shifts": shifts}


def reference(greens, derivative, phonon, mode_index, neighbours, counts, shifts):
    live_mask = jnp.arange(NB, dtype=jnp.int32)[None, :] < counts[:, None]
    coupling = phonon[:, mode_index]
    gradients = derivative.astype(jnp.float32)
    weighted = coupling[:, :, :, 0, :, None, None] * gradients[None, :, :, 0, None, :, :]
    for direction in range(1, 3):
        weighted = weighted + coupling[:, :, :, direction, :, None, None] * gradients[None, :, :, direction, None, :, :]
    weighted = weighted.astype(jnp.bfloat16)

    def per_energy(energy_blocks):
        rounded = energy_blocks.astype(jnp.bfloat16)[neighbours]
        right_side = jnp.einsum("akcpq,akjrq->akjcpr", rounded.astype(jnp.float32), gradients).astype(jnp.bfloat16)
        products = jnp.einsum("makjpq,akjcqr->makcpr", weighted.astype(jnp.float32), right_side.astype(jnp.float32))
        products = jnp.where(live_mask[None, :, :, None, None, None], products, jnp.float32(0.0))
        return jnp.sum(products, axis=2)

    source_terms = lax.map(per_energy, greens)
    upper_terms = source_terms[:, 0]
    lower_terms = source_terms[:, 1]
    padding = jnp.zeros_like(upper_terms)
    from_above = lax.dynamic_slice_in_dim(jnp.concatenate([upper_terms, padding], axis=0), shifts[0].astype(jnp.int32), ENERGIES, 0)
    from_below = lax.dynamic_slice_in_dim(jnp.concatenate([padding, lower_terms], axis=0), (ENERGIES - shifts[1]).astype(jnp.int32), ENERGIES, 0)
    return from_above + from_below
```

```python
import functools

import jax
import jax.numpy as jnp
from jax import lax
from jax.experimental import pallas as pl
from jax.experimental.pallas import tpu as pltpu
from jax.sharding import PartitionSpec as P

MESH = pl.DeviceIdType.MESH

LINES = {
    (1, 2): (1, 2, 3, 0),
    (1, 3): (1, 2, 3, 0),
    (2, 1): (0, 3, 1, 2),
    (2, 3): (2, 3, None, 0),
    (3, 1): (3, 0, 1, 2),
    (3, 2): (3, None, 0, 1),
}


def plan_of(first, second, energies=4):
    lines = LINES[(first, second)]
    needs = []
    for e in range(energies):
        up, low = e + first, e - second
        needs.append((up if up < energies else None, low if low >= 0 else None))
    roles, shares = [], []
    for d, carried in enumerate(lines):
        if carried is not None and carried in needs[d]:
            roles.append(needs[d].index(carried))
        else:
            roles.append(0 if needs[d][0] is None else 1)
    for d in range(energies):
        for term in range(2):
            want = needs[d][term]
            if want is None or (roles[d] == term and lines[d] == want):
                continue
            assert lines[d] is None or roles[d] != term
            shares.append((lines.index(want), d, term))
    return lines, roles, shares


def gather_kernel(plan, greens_ref, out_ref, own, local_sem, send_init, recv_init, send_z, recv_z, send_share, recv_share):
    lines, roles, shares = plan
    energies = len(lines)
    groups = own.shape[0]
    e = lax.axis_index("energy")
    z = lax.axis_index("orb")
    peers = lax.axis_size("orb")

    barrier = pltpu.get_barrier_semaphore()
    for step in range(1, energies):
        pl.semaphore_signal(
            barrier, inc=1, device_id={"energy": lax.rem(e + step, energies)}, device_id_type=MESH
        )

    @pl.when(z > 0)
    def _():
        pl.semaphore_signal(barrier, inc=1, device_id={"orb": z - 1}, device_id_type=MESH)

    @pl.when(z < peers - 1)
    def _():
        pl.semaphore_signal(barrier, inc=1, device_id={"orb": z + 1}, device_id_type=MESH)

    own[...] = greens_ref[0].astype(own.dtype)
    inner = jnp.minimum(z, 1) + jnp.minimum(peers - 1 - z, 1)
    pl.semaphore_wait(barrier, energies - 1 + inner)

    def at(role, source, c):
        return out_ref.at[role, source * groups + c]

    def init_copy(d, c):
        return pltpu.make_async_remote_copy(
            src_ref=own.at[c], dst_ref=at(roles[d], z, c),
            send_sem=send_init.at[c], recv_sem=recv_init.at[c],
            device_id={"energy": d}, device_id_type=MESH,
        )

    def local_copy(d, c):
        return pltpu.make_async_copy(own.at[c], at(roles[d], z, c), local_sem.at[c])

    for d, carried in enumerate(lines):
        if carried is None:
            continue

        @pl.when(e == carried)
        def _():
            for c in range(groups):
                (local_copy if d == carried else init_copy)(d, c).start()

    def line(d):
        role = roles[d]
        users = [(to, term) for (by, to, term) in shares if by == d]

        def z_copy(source, c, way):
            return pltpu.make_async_remote_copy(
                src_ref=at(role, source, c), dst_ref=at(role, source, c),
                send_sem=send_z.at[way, source, c], recv_sem=recv_z.at[source, c],
                device_id={"orb": z + (1 if way else -1)}, device_id_type=MESH,
            )

        def share_copy(source, c, i):
            to, term = users[i]
            return pltpu.make_async_remote_copy(
                src_ref=at(role, source, c), dst_ref=at(term, source, c),
                send_sem=send_share.at[i, source, c], recv_sem=recv_share.at[source, c],
                device_id={"energy": to}, device_id_type=MESH,
            )

        def spread(source, c, ways):
            for way in ways:
                @pl.when(z < peers - 1 if way else z > 0)
                def _():
                    z_copy(source, c, way).start()
            for i in range(len(users)):
                share_copy(source, c, i).start()

        for c in range(groups):
            if lines[d] == d:
                local_copy(d, c).wait()
            else:
                init_copy(d, c).wait_recv()
            spread(z, c, (0, 1))
        for distance in range(1, peers):
            for c in range(groups):
                @pl.when(z - distance >= 0)
                def _():
                    z_copy(z - distance, c, 0).wait_recv()
                    spread(z - distance, c, (1,))

                @pl.when(z + distance < peers)
                def _():
                    z_copy(z + distance, c, 0).wait_recv()
                    spread(z + distance, c, (0,))
        for distance in range(peers):
            for c in range(groups):
                @pl.when((z - distance >= 0) & (z < peers - 1))
                def _():
                    z_copy(z - distance, c, 1).wait_send()

                @pl.when((z + distance < peers) & (z > 0))
                def _():
                    z_copy(z + distance, c, 0).wait_send()
        for i in range(len(users)):
            for source in range(peers):
                for c in range(groups):
                    share_copy(source, c, i).wait_send()

    for d in range(energies):
        if lines[d] is not None:
            pl.when(e == d)(functools.partial(line, d))
    for by, to, term in shares:
        @pl.when(e == to)
        def _():
            for source in range(peers):
                for c in range(groups):
                    pltpu.make_async_remote_copy(
                        src_ref=at(term, source, c), dst_ref=at(term, source, c),
                        send_sem=send_share.at[0, source, c], recv_sem=recv_share.at[source, c],
                        device_id={"energy": by}, device_id_type=MESH,
                    ).wait_recv()
    for d, carried in enumerate(lines):
        if carried is None or carried == d:
            continue

        @pl.when(e == carried)
        def _():
            for c in range(groups):
                init_copy(d, c).wait_send()


def gather_direct(first, second, number, greens):
    plan = plan_of(first, second)
    peers = lax.axis_size("orb")
    groups = greens.shape[1]
    users = max([1] + [sum(1 for s in plan[2] if s[0] == d) for d in range(4)])
    sem = pltpu.SemaphoreType.DMA
    return pl.pallas_call(
        functools.partial(gather_kernel, plan),
        out_shape=jax.ShapeDtypeStruct((2, peers * groups) + greens.shape[2:], jnp.bfloat16),
        in_specs=[pl.BlockSpec(memory_space=pltpu.VMEM)],
        out_specs=pl.BlockSpec(memory_space=pl.ANY),
        scratch_shapes=[
            pltpu.VMEM(greens.shape[1:], jnp.bfloat16),
            sem((groups,)), sem((groups,)), sem((groups,)),
            sem((2, peers, groups)), sem((peers, groups)),
            sem((users, peers, groups)), sem((peers, groups)),
        ],
        compiler_params=pltpu.CompilerParams(
            collective_id=number, has_side_effects=True, vmem_limit_bytes=16 * 2**20
        ),
        name="gather_%d_%d" % (first, second),
    )(greens)


def shifted(values, amount, sign):
    size = lax.axis_size("energy")
    for section in range((size - 1).bit_length()):
        by = sign * (1 << section)
        pairs = [(i, i + by) for i in range(size) if 0 <= i + by < size]
        moved = lax.ppermute(values, "energy", pairs)
        values = jnp.where(jnp.right_shift(amount, section) & 1 == 1, moved, values)
    return values


def gather_general(greens, shifts):
    own = greens[0].astype(jnp.bfloat16)
    pair = jnp.stack([shifted(own, shifts[0], -1), shifted(own, shifts[1], 1)])
    return lax.all_gather(pair, "orb", axis=1, tiled=True)


def gathered_blocks(greens, shifts):
    if lax.axis_size("energy") != 4:
        return gather_general(greens, shifts)
    combos = sorted(LINES)
    which = sum(
        jnp.where((shifts[0] == a) & (shifts[1] == b), i, 0) for i, (a, b) in enumerate(combos)
    )
    branches = [functools.partial(gather_direct, a, b, i) for i, (a, b) in enumerate(combos)]
    return lax.switch(which, branches, greens)


def terms_kernel(fanout, table_ref, phonon_ref, blocks_ref, gradient_ref, out_ref):
    a = pl.program_id(0)
    slots = pl.num_programs(0) * fanout
    no = out_ref.shape[-1]
    count = table_ref[2 * slots + a]
    flags = 2 * slots + pl.num_programs(0)
    out_ref[...] = jnp.zeros_like(out_ref)

    def term(m):
        total = jnp.zeros((no, 2 * no), jnp.float32)
        for k in range(fanout):
            slot = a * fanout + k
            group = table_ref[slot]
            mode = table_ref[slots + slot]
            live = jnp.where(k < count, jnp.float32(1), jnp.float32(0))
            grads = gradient_ref[0, k]
            wide = grads.astype(jnp.float32)
            weights = []
            for j in range(3):
                w = (phonon_ref[m, mode * 9 + j] * live) * wide[0]
                for i in range(1, 3):
                    w = w + (phonon_ref[m, mode * 9 + 3 * i + j] * live) * wide[i]
                weights.append(w.astype(jnp.bfloat16))
            green = blocks_ref[m, group].reshape(2 * no, no)
            right = lax.dot_general(
                green, grads.reshape(3 * no, no), (((1,), (1,)), ((), ())),
                preferred_element_type=jnp.float32,
            ).astype(jnp.bfloat16)
            stacked = jnp.concatenate(
                [
                    jnp.concatenate(
                        [right[c * no:(c + 1) * no, j * no:(j + 1) * no] for c in range(2)], axis=1
                    )
                    for j in range(3)
                ],
                axis=0,
            )
            total = total + jnp.dot(
                jnp.concatenate(weights, axis=1), stacked, preferred_element_type=jnp.float32
            )
        for c in range(2):
            out_ref[0, 0, c] += total[:, c * no:(c + 1) * no]

    for m in range(2):
        pl.when(table_ref[flags + m] == 1)(functools.partial(term, m))


def body(greens, derivative, phonon, mode_index, neighbours, counts, shifts):
    groups, fanout, _, no, _ = derivative.shape
    me, energy = lax.axis_index("orb"), lax.axis_index("energy")
    blocks = gathered_blocks(greens, shifts)
    here = jnp.stack([energy + shifts[0] < lax.axis_size("energy"), energy - shifts[1] >= 0])
    table = jnp.concatenate([
        lax.dynamic_slice_in_dim(neighbours, me * groups, groups, 0).reshape(-1),
        mode_index.reshape(-1),
        lax.dynamic_slice_in_dim(counts, me * groups, groups, 0),
        here.astype(jnp.int32),
    ])
    return pl.pallas_call(
        functools.partial(terms_kernel, fanout),
        grid_spec=pltpu.PrefetchScalarGridSpec(
            num_scalar_prefetch=1,
            grid=(groups,),
            in_specs=[
                pl.BlockSpec(memory_space=pltpu.SMEM),
                pl.BlockSpec(memory_space=pltpu.VMEM),
                pl.BlockSpec((1,) + derivative.shape[1:], lambda a, _: (a, 0, 0, 0, 0)),
            ],
            out_specs=pl.BlockSpec((1, 1, 2, no, no), lambda a, _: (0, a, 0, 0, 0)),
        ),
        out_shape=jax.ShapeDtypeStruct(greens.shape, jnp.float32),
        compiler_params=pltpu.CompilerParams(vmem_limit_bytes=48 * 2**20),
        name="terms",
    )(table, phonon.reshape(2, -1), blocks, derivative)


def solution(mesh):
    in_specs = (
        P(("parts", "energy"), "orb", None, None, None),
        P("orb", None, None, None, None),
        P(),
        P("orb", None),
        P(),
        P(),
        P(),
    )
    out_specs = P(("parts", "energy"), "orb", None, None, None)
    return jax.shard_map(body, mesh=mesh, in_specs=in_specs, out_specs=out_specs, check_vma=False)
```

```python
import functools

import jax
import jax.numpy as jnp
from jax import lax
from jax.experimental import pallas as pl
from jax.experimental.pallas import tpu as pltpu
from jax.sharding import PartitionSpec as P

MESH = pl.DeviceIdType.MESH

LINES = {
    (1, 2): (1, 2, 3, 0),
    (1, 3): (1, 2, 3, 0),
    (2, 1): (0, 3, 1, 2),
    (2, 3): (2, 3, None, 0),
    (3, 1): (3, 0, 1, 2),
    (3, 2): (3, None, 0, 1),
}


def plan_of(first, second, energies=4):
    lines = LINES[(first, second)]
    needs = []
    for e in range(energies):
        up, low = e + first, e - second
        needs.append((up if up < energies else None, low if low >= 0 else None))
    roles, shares = [], []
    for d, carried in enumerate(lines):
        if carried is not None and carried in needs[d]:
            roles.append(needs[d].index(carried))
        else:
            roles.append(0 if needs[d][0] is None else 1)
    for d in range(energies):
        for term in range(2):
            want = needs[d][term]
            if want is None or (roles[d] == term and lines[d] == want):
                continue
            assert lines[d] is None or roles[d] != term
            shares.append((lines.index(want), d, term))
    return lines, roles, shares


def gather_kernel(plan, greens_ref, out_ref, own, local_sem, send_init, recv_init, send_z, recv_z, send_share, recv_share):
    lines, roles, shares = plan
    energies = len(lines)
    groups = own.shape[0]
    e = lax.axis_index("energy")
    z = lax.axis_index("orb")
    peers = lax.axis_size("orb")

    barrier = pltpu.get_barrier_semaphore()
    for step in range(1, energies):
        pl.semaphore_signal(
            barrier, inc=1, device_id={"energy": lax.rem(e + step, energies)}, device_id_type=MESH
        )

    @pl.when(z > 0)
    def _():
        pl.semaphore_signal(barrier, inc=1, device_id={"orb": z - 1}, device_id_type=MESH)

    @pl.when(z < peers - 1)
    def _():
        pl.semaphore_signal(barrier, inc=1, device_id={"orb": z + 1}, device_id_type=MESH)

    own[...] = greens_ref[0].astype(own.dtype)
    inner = jnp.minimum(z, 1) + jnp.minimum(peers - 1 - z, 1)
    pl.semaphore_wait(barrier, energies - 1 + inner)

    def at(role, source, c):
        return out_ref.at[role, source * groups + c]

    def init_copy(d, c):
        return pltpu.make_async_remote_copy(
            src_ref=own.at[c], dst_ref=at(roles[d], z, c),
            send_sem=send_init.at[c], recv_sem=recv_init.at[c],
            device_id={"energy": d}, device_id_type=MESH,
        )

    def local_copy(d, c):
        return pltpu.make_async_copy(own.at[c], at(roles[d], z, c), local_sem.at[c])

    for d, carried in enumerate(lines):
        if carried is None:
            continue

        @pl.when(e == carried)
        def _():
            for c in range(groups):
                (local_copy if d == carried else init_copy)(d, c).start()

    def line(d):
        role = roles[d]
        users = [(to, term) for (by, to, term) in shares if by == d]

        def z_copy(source, c, way):
            return pltpu.make_async_remote_copy(
                src_ref=at(role, source, c), dst_ref=at(role, source, c),
                send_sem=send_z.at[way, source, c], recv_sem=recv_z.at[source, c],
                device_id={"orb": z + (1 if way else -1)}, device_id_type=MESH,
            )

        def share_copy(source, c, i):
            to, term = users[i]
            return pltpu.make_async_remote_copy(
                src_ref=at(role, source, c), dst_ref=at(term, source, c),
                send_sem=send_share.at[i, source, c], recv_sem=recv_share.at[source, c],
                device_id={"energy": to}, device_id_type=MESH,
            )

        def spread(source, c, ways):
            for way in ways:
                @pl.when(z < peers - 1 if way else z > 0)
                def _():
                    z_copy(source, c, way).start()
            for i in range(len(users)):
                share_copy(source, c, i).start()

        for c in range(groups):
            if lines[d] == d:
                local_copy(d, c).wait()
            else:
                init_copy(d, c).wait_recv()
            spread(z, c, (0, 1))
        for distance in range(1, peers):
            for c in range(groups):
                @pl.when(z - distance >= 0)
                def _():
                    z_copy(z - distance, c, 0).wait_recv()
                    spread(z - distance, c, (1,))

                @pl.when(z + distance < peers)
                def _():
                    z_copy(z + distance, c, 0).wait_recv()
                    spread(z + distance, c, (0,))
        for distance in range(peers):
            for c in range(groups):
                @pl.when((z - distance >= 0) & (z < peers - 1))
                def _():
                    z_copy(z - distance, c, 1).wait_send()

                @pl.when((z + distance < peers) & (z > 0))
                def _():
                    z_copy(z + distance, c, 0).wait_send()
        for i in range(len(users)):
            for source in range(peers):
                for c in range(groups):
                    share_copy(source, c, i).wait_send()

    for d in range(energies):
        if lines[d] is not None:
            pl.when(e == d)(functools.partial(line, d))
    for by, to, term in shares:
        @pl.when(e == to)
        def _():
            for source in range(peers):
                for c in range(groups):
                    pltpu.make_async_remote_copy(
                        src_ref=at(term, source, c), dst_ref=at(term, source, c),
                        send_sem=send_share.at[0, source, c], recv_sem=recv_share.at[source, c],
                        device_id={"energy": by}, device_id_type=MESH,
                    ).wait_recv()
    for d, carried in enumerate(lines):
        if carried is None or carried == d:
            continue

        @pl.when(e == carried)
        def _():
            for c in range(groups):
                init_copy(d, c).wait_send()


def gather_direct(first, second, number, greens):
    plan = plan_of(first, second)
    peers = lax.axis_size("orb")
    groups = greens.shape[1]
    users = max([1] + [sum(1 for s in plan[2] if s[0] == d) for d in range(4)])
    sem = pltpu.SemaphoreType.DMA
    return pl.pallas_call(
        functools.partial(gather_kernel, plan),
        out_shape=jax.ShapeDtypeStruct((2, peers * groups) + greens.shape[2:], jnp.bfloat16),
        in_specs=[pl.BlockSpec(memory_space=pltpu.VMEM)],
        out_specs=pl.BlockSpec(memory_space=pltpu.VMEM),
        scratch_shapes=[
            pltpu.VMEM(greens.shape[1:], jnp.bfloat16),
            sem((groups,)), sem((groups,)), sem((groups,)),
            sem((2, peers, groups)), sem((peers, groups)),
            sem((users, peers, groups)), sem((peers, groups)),
        ],
        compiler_params=pltpu.CompilerParams(
            collective_id=number, has_side_effects=True, vmem_limit_bytes=16 * 2**20
        ),
        name="gather_%d_%d" % (first, second),
    )(greens)


def shifted(values, amount, sign):
    size = lax.axis_size("energy")
    for section in range((size - 1).bit_length()):
        by = sign * (1 << section)
        pairs = [(i, i + by) for i in range(size) if 0 <= i + by < size]
        moved = lax.ppermute(values, "energy", pairs)
        values = jnp.where(jnp.right_shift(amount, section) & 1 == 1, moved, values)
    return values


def gather_general(greens, shifts):
    own = greens[0].astype(jnp.bfloat16)
    pair = jnp.stack([shifted(own, shifts[0], -1), shifted(own, shifts[1], 1)])
    return lax.all_gather(pair, "orb", axis=1, tiled=True)


def clear(out_ref):
    out_ref[...] = jnp.zeros_like(out_ref)


def terms_kernel(fanout, names_ref, modes_ref, counts_ref, shifts_ref, phonon_ref, blocks_ref, gradient_ref, out_ref):
    a = pl.program_id(0)
    energy, reader = lax.axis_index("energy"), lax.axis_index("orb") * pl.num_programs(0) + a
    no = out_ref.shape[-1]
    count = counts_ref[reader]

    def terms(chosen):
        weights, rights = [], []
        for k in range(fanout):
            group = names_ref[reader, k]
            mode = modes_ref[a, k]
            live = jnp.where(k < count, jnp.float32(1), jnp.float32(0))
            grads = gradient_ref[0, k]
            wide = grads.astype(jnp.float32)
            for m in chosen:
                for j in range(3):
                    w = (phonon_ref[m, mode * 9 + j] * live) * wide[0]
                    for i in range(1, 3):
                        w = w + (phonon_ref[m, mode * 9 + 3 * i + j] * live) * wide[i]
                    weights.append(w.astype(jnp.bfloat16))
            green = jnp.concatenate(
                [blocks_ref[m, group].reshape(2 * no, no) for m in chosen], axis=0
            )
            right = lax.dot_general(
                green, grads.reshape(3 * no, no), (((1,), (1,)), ((), ())),
                preferred_element_type=jnp.float32,
            ).astype(jnp.bfloat16)
            for n in range(len(chosen)):
                for j in range(3):
                    rights.append(
                        jnp.concatenate(
                            [
                                right[(2 * n + c) * no:(2 * n + c + 1) * no, j * no:(j + 1) * no]
                                for c in range(2)
                            ],
                            axis=1,
                        )
                    )
        total = jnp.dot(
            jnp.concatenate(weights, axis=1), jnp.concatenate(rights, axis=0),
            preferred_element_type=jnp.float32,
        )
        for c in range(2):
            out_ref[0, 0, c] = total[:, c * no:(c + 1) * no]

    upper = energy + shifts_ref[0] < lax.axis_size("energy")
    lower = energy - shifts_ref[1] >= 0
    pl.when(upper & lower)(functools.partial(terms, (0, 1)))
    pl.when(upper & ~lower)(functools.partial(terms, (0,)))
    pl.when(lower & ~upper)(functools.partial(terms, (1,)))
    pl.when(~(upper | lower))(functools.partial(clear, out_ref))


def products(derivative, phonon, tables, blocks):
    groups, fanout, _, no, _ = derivative.shape
    return pl.pallas_call(
        functools.partial(terms_kernel, fanout),
        grid_spec=pltpu.PrefetchScalarGridSpec(
            num_scalar_prefetch=4,
            grid=(groups,),
            in_specs=[
                pl.BlockSpec(memory_space=pltpu.SMEM),
                pl.BlockSpec(memory_space=pltpu.VMEM),
                pl.BlockSpec((1,) + derivative.shape[1:], lambda a, *_: (a, 0, 0, 0, 0)),
            ],
            out_specs=pl.BlockSpec((1, 1, 2, no, no), lambda a, *_: (0, a, 0, 0, 0)),
        ),
        out_shape=jax.ShapeDtypeStruct((1, groups, 2, no, no), jnp.float32),
        compiler_params=pltpu.CompilerParams(vmem_limit_bytes=40 * 2**20),
        name="terms",
    )(*tables, phonon, blocks, derivative)


def direct(first, second, number, greens, derivative, phonon, *tables):
    return products(derivative, phonon, tables, gather_direct(first, second, number, greens))


def body(greens, derivative, phonon, mode_index, neighbours, counts, shifts):
    tables = (neighbours, mode_index, counts, shifts)
    phonon = phonon.reshape(2, -1)
    if lax.axis_size("energy") != 4:
        return products(derivative, phonon, tables, gather_general(greens, shifts))
    combos = sorted(LINES)
    first, second = shifts[0], shifts[1]
    which = 2 * first + second - 3 - (second > first).astype(jnp.int32)
    branches = [functools.partial(direct, a, b, i) for i, (a, b) in enumerate(combos)]
    return lax.switch(which, branches, greens, derivative, phonon, *tables)


def solution(mesh):
    in_specs = (
        P(("parts", "energy"), "orb", None, None, None),
        P("orb", None, None, None, None),
        P(),
        P("orb", None),
        P(),
        P(),
        P(),
    )
    out_specs = P(("parts", "energy"), "orb", None, None, None)
    return jax.shard_map(body, mesh=mesh, in_specs=in_specs, out_specs=out_specs, check_vma=False)
```
